32 devices in a mesh: row: 8 (over z, y), col: 4 (over x, core).
Axes of the slice: x: 2, y: 2, z: 4, core: 2. Of those that a mesh axis runs over, the one named last changes fastest.
Arguments:
- features: float32 [16384, 512], P(('row', 'col')), may hold values from -6 to 6
- tiles: float32 [8, 4, 128, 128, 128], P('row', 'col'), may hold values from -0.4 to 0.4
- tile_rows: int32 [8, 4, 128], P('row', 'col'), may hold values from 0 to 15
- tile_cols: int32 [8, 4, 128], P('row', 'col'), may hold values from 0 to 15
- tile_count: int32 [8, 4], P('row', 'col'), may hold values from 16 to 128, as said below
- needed: int32 [8, 4, 8, 2], P('row', 'col'), may hold values from 0 to 3, as said below
- w_in: bfloat16 [512, 2048], replicated, may hold values from -0.25 to 0.25
- bias_in: float32 [2048], replicated, may hold values from -5 to 5
- w_out: bfloat16 [2048, 512], replicated, may hold values from -0.125 to 0.125
- bias_out: float32 [512], replicated, may hold values from -5 to 5
Outputs:
- updated: bfloat16 [16384, 512], P(('row', 'col'))
The draws below stay inside these ranges and needn't reach their ends.
Inputs may be any that keep to these rules, and one draw needn't show every extreme that they name: tile_count of every grid cell lies between 16 and 64, except one cell of each draw that has all 128 tiles live. Each list needed[r, c, q] holds 2 different block numbers.
All inputs are finite; a program needn't handle non-finite values.
Results may differ from the reference program's by a relative error of at most 0.0054.
Values sent between devices are 32-bit elements; how exact they have to be, the bound alone decides.
A program may use at most 128 MiB of HBM per device.

```python
import jax
import jax.numpy as jnp
from jax import lax

F = 512
HID = 2048
TILE = 128
BPS = 4
TPD = 128
MAXB = 2
GRID_R = 8
GRID_C = 4
NODES = 16384


def draw_needed(key, part):
    scores = jax.random.randint(jax.random.fold_in(key, 11), (GRID_R, GRID_C, GRID_R, BPS), 0, 1 << 20)
    scores = scores * BPS + jnp.arange(BPS, dtype=jnp.int32)
    order = jnp.argsort(scores, axis=-1)
    return order[..., :MAXB].astype(jnp.int32)


def draw_tile_count(key, part):
    first = jax.random.fold_in(key, 23)
    second = jax.random.fold_in(key, 29)
    base = jax.random.randint(first, (GRID_R * GRID_C,), TPD // 8, TPD // 2 + 1)
    chosen = jax.random.randint(second, (), 0, GRID_R * GRID_C)
    filled = jnp.where(jnp.arange(GRID_R * GRID_C) == chosen, TPD, base)
    return filled.reshape(GRID_R, GRID_C).astype(jnp.int32)


def place_ends(entries, stream_key, smallest, top_value):
    longest = entries.shape.index(max(entries.shape))
    spots = []
    for shift in (0, 1):
        where = [jax.random.randint(jax.random.fold_in(stream_key, axis), (), 0, length) for axis, length in enumerate(entries.shape)]
        where[longest] = (where[longest] + shift) % entries.shape[longest]
        spots.append(tuple(where))
    return entries.at[spots[0]].set(smallest).at[spots[1]].set(top_value)


def levels(own_key, shape, split, least, largest):
    def one(axis_at, blocks):
        heights = jax.random.uniform(jax.random.fold_in(jax.random.fold_in(own_key, 6), axis_at), (blocks,), jnp.float32, least / len(split), largest / len(split))
        return jnp.repeat(jnp.exp(heights), shape[axis_at] // blocks).reshape((-1,) + (1,) * (len(shape) - axis_at - 1))

    factor_of = one(*split[0])
    for cut in split[1:]:
        factor_of = factor_of * one(*cut)
    return factor_of


def bell_draw(rng, dims, scale, bound, pieces=(), held_as=jnp.bfloat16):
    drawn = scale * jax.random.normal(rng, dims, jnp.float32)
    if pieces:
        drawn = drawn * levels(rng, dims, pieces, -0.22, 0.18)
    return jnp.clip(drawn, -bound, bound).astype(held_as)


def setup_inputs(seed: int = 0) -> dict:
    arg_keys = jax.random.split(jax.random.key(seed), 11)
    features = bell_draw(arg_keys[0], (NODES, F), 1.0, 6.0, ((0, 32),), jnp.float32)
    tiles = bell_draw(arg_keys[1], (GRID_R, GRID_C, TPD, TILE, TILE), 0.05, 0.4, ((0, 8), (1, 4)), jnp.float32)
    tile_rows = place_ends(jax.random.randint(arg_keys[2], (GRID_R, GRID_C, TPD), 0, GRID_C * BPS), jax.random.fold_in(arg_keys[2], 1), 0, (GRID_C * BPS) - 1).astype(jnp.int32)
    tile_cols = place_ends(jax.random.randint(arg_keys[3], (GRID_R, GRID_C, TPD), 0, GRID_R * MAXB), jax.random.fold_in(arg_keys[3], 1), 0, (GRID_R * MAXB) - 1).astype(jnp.int32)
    tile_count = draw_tile_count(jax.random.fold_in(arg_keys[10], 71), 0)
    needed = draw_needed(jax.random.fold_in(arg_keys[10], 71), 0)
    w_in = bell_draw(arg_keys[6], (F, HID), F ** -0.5, 0.25)
    bias_in = bell_draw(arg_keys[7], (HID,), 1.0, 5.0, (), jnp.float32)
    w_out = bell_draw(arg_keys[8], (HID, F), HID ** -0.5, 0.125)
    bias_out = bell_draw(arg_keys[9], (F,), 1.0, 5.0, (), jnp.float32)
    return {"features": features, "tiles": tiles, "tile_rows": tile_rows, "tile_cols": tile_cols, "tile_count": tile_count, "needed": needed, "w_in": w_in, "bias_in": bias_in, "w_out": w_out, "bias_out": bias_out}


def reference(features, tiles, tile_rows, tile_cols, tile_count, needed, w_in, bias_in, w_out, bias_out):
    blocks = features.reshape(-1, TILE, F)
    row_blocks = GRID_C * BPS

    def cell(total, position):
        grid_row = position // GRID_C
        grid_col = position % GRID_C
        column_slot = tile_cols[grid_row, grid_col]
        source = column_slot // MAXB
        local = needed[grid_row, grid_col].reshape(-1)[column_slot]
        source_block = ((source * GRID_C + grid_col) * BPS + local).astype(jnp.int32)
        target_block = (grid_row * row_blocks + tile_rows[grid_row, grid_col]).astype(jnp.int32)
        live = (jnp.arange(TPD) < tile_count[grid_row, grid_col]).astype(jnp.float32)
        inputs = blocks[source_block]
        product = jnp.einsum("tpq,tqf->tpf", tiles[grid_row, grid_col], inputs, precision=lax.Precision.HIGHEST)
        product = product * live[:, None, None]
        return total.at[target_block].add(product), None

    aggregate, _ = lax.scan(cell, jnp.zeros(blocks.shape, jnp.float32), jnp.arange(GRID_R * GRID_C, dtype=jnp.int32))
    aggregate = aggregate.reshape(features.shape)
    mixed = (1.25 * features + aggregate).astype(jnp.bfloat16)
    hidden = jax.nn.relu(jnp.dot(mixed, w_in, preferred_element_type=jnp.float32) + bias_in).astype(jnp.bfloat16)
    return (jnp.dot(hidden, w_out, preferred_element_type=jnp.float32) + bias_out).astype(jnp.bfloat16)
```

```python
import functools
import math

import jax
import jax.numpy as jnp
from jax import lax
from jax.experimental import pallas as pl
from jax.experimental.pallas import tpu as pltpu
from jax.sharding import PartitionSpec as P

gin_epsilon = 0.25
MESH = pl.DeviceIdType.MESH
MIB = 1 << 20


def assemble_kernel(rows, cols, count, tiles_ref, out_ref, acc):
    edge = tiles_ref.shape[-1]
    group = acc.shape[0] // edge
    first = pl.program_id(0) * group
    acc[...] = jnp.zeros_like(acc)

    def add(t, carry):
        local = rows[t] - first

        @pl.when((local >= 0) & (local < group))
        def _():
            at_row = pl.multiple_of(local * edge, edge)
            at_col = pl.multiple_of(cols[t] * edge, edge)
            acc[pl.ds(at_row, edge), pl.ds(at_col, edge)] += tiles_ref[t]

        return carry

    lax.fori_loop(0, count[0], add, 0)
    out_ref[...] = acc[...].astype(jnp.bfloat16)


def assemble(tiles, rows, cols, count, targets, slots):
    total, edge, _ = tiles.shape
    groups = max(1, targets * slots * edge * edge * 4 // (8 * MIB))
    height = targets // groups * edge
    return pl.pallas_call(
        assemble_kernel,
        out_shape=jax.ShapeDtypeStruct((targets * edge, slots * edge), jnp.bfloat16),
        grid_spec=pltpu.PrefetchScalarGridSpec(
            num_scalar_prefetch=3,
            grid=(groups,),
            in_specs=[pl.BlockSpec(memory_space=pltpu.VMEM)],
            out_specs=pl.BlockSpec((height, slots * edge), lambda g, *_: (g, 0)),
            scratch_shapes=[pltpu.VMEM((height, slots * edge), jnp.float32)],
        ),
        compiler_params=pltpu.CompilerParams(vmem_limit_bytes=40 * MIB),
        name="assemble",
    )(rows, cols, count, tiles)


def layer_kernel(
    cfg,
    features,
    wanted,
    dense,
    w_in,
    bias_in,
    w_out,
    bias_out,
    out,
    zbuf,
    ysend_buf,
    yrecv_buf,
    asked,
    panels,
    pool,
    partial,
    core_buf,
    x_buf,
    w_in_v,
    w_out_v,
    mixed,
    feat_sem,
    dense_sem,
    w_sem,
    z_recv,
    right_send,
    left_send,
    y_send,
    y_recv,
    ask_send,
    ask_recv,
    core_send,
    core_recv,
    x_send,
    x_recv,
):
    Z, Y, X, J, B, edge, width, chunks, resident = cfg
    owners = 2 * X
    nodes = B * edge
    row, col = lax.axis_index("row"), lax.axis_index("col")
    z, y = row // Y, lax.rem(row, Y)
    x, core = col // 2, lax.rem(col, 2)
    mate = 1 - core

    def turn(base, step, size):
        return lax.rem(base + step + size, size)

    def at_z(other):
        return (other * Y + y, col)

    def at_y(other):
        return (z * Y + other, col)

    def at_x(other, which):
        return (row, other * 2 + which)

    def local_features(k):
        return pltpu.make_async_copy(
            features.at[:, pl.ds(pl.multiple_of(k * width, width), width)],
            zbuf.at[k, z],
            feat_sem.at[k],
        )

    def z_copy(k, source, to, sem):
        return pltpu.make_async_remote_copy(
            src_ref=zbuf.at[k, source],
            dst_ref=zbuf.at[k, source],
            send_sem=sem.at[k, source],
            recv_sem=z_recv.at[k, source],
            device_id=at_z(to),
            device_id_type=MESH,
        )

    def to_right(k, source):
        return z_copy(k, source, z + 1, right_send)

    def to_left(k, source):
        return z_copy(k, source, z - 1, left_send)

    def ask_copy(d):
        return pltpu.make_async_remote_copy(
            src_ref=wanted,
            dst_ref=asked.at[d - 1],
            send_sem=ask_send.at[d - 1],
            recv_sem=ask_recv.at[d - 1],
            device_id=at_y(turn(y, d, Y)),
            device_id_type=MESH,
        )

    def y_copy(k, d, source):
        return pltpu.make_async_remote_copy(
            src_ref=ysend_buf.at[k, d - 1, source],
            dst_ref=yrecv_buf.at[k, d - 1, source],
            send_sem=y_send.at[k, d - 1, source],
            recv_sem=y_recv.at[k, d - 1, source],
            device_id=at_y(turn(y, -d, Y)),
            device_id_type=MESH,
        )

    def core_copy(k, other):
        return pltpu.make_async_remote_copy(
            src_ref=partial.at[k, other * 2 + mate],
            dst_ref=core_buf.at[k, other],
            send_sem=core_send.at[k, other],
            recv_sem=core_recv.at[k, other],
            device_id=at_x(x, mate),
            device_id_type=MESH,
        )

    def x_copy(k, d):
        other = turn(x, d, X)
        return pltpu.make_async_remote_copy(
            src_ref=partial.at[k, other * 2 + core],
            dst_ref=x_buf.at[k, d - 1],
            send_sem=x_send.at[k, d - 1],
            recv_sem=x_recv.at[k, d - 1],
            device_id=at_x(other, core),
            device_id_type=MESH,
        )

    def load_dense(p, slot, sem):
        return pltpu.make_async_copy(
            dense.at[pl.ds(p * nodes, nodes), :], panels.at[slot], dense_sem.at[sem]
        )

    def load_weights():
        return (
            pltpu.make_async_copy(w_in, w_in_v, w_sem.at[0]),
            pltpu.make_async_copy(w_out, w_out_v, w_sem.at[1]),
        )

    def pick(k, source, row_list):
        name = jnp.broadcast_to(row_list, (edge, width))
        value = zbuf[k, source, pl.ds(0, edge), :]
        for b in range(1, B):
            value = jnp.where(name == b, zbuf[k, source, pl.ds(b * edge, edge), :], value)
        return value

    def send_y(k, source):
        for d in range(1, Y):
            for j in range(J):
                entry = (source * Y + y) * J + j
                ysend_buf[k, d - 1, source, pl.ds(j * edge, edge), :] = pick(
                    k, source, asked[d - 1, pl.ds(entry, 1), :]
                )
            y_copy(k, d, source).start()

    def send_own(k):
        local_features(k).wait()

        @pl.when(z < Z - 1)
        def _():
            to_right(k, z).start()

        @pl.when(z > 0)
        def _():
            to_left(k, z).start()

    for k in range(chunks):
        local_features(k).start()
    barrier = pltpu.get_barrier_semaphore()

    @pl.when(z < Z - 1)
    def _():
        pl.semaphore_signal(barrier, inc=1, device_id=at_z(z + 1), device_id_type=MESH)

    @pl.when(z > 0)
    def _():
        pl.semaphore_signal(barrier, inc=1, device_id=at_z(z - 1), device_id_type=MESH)

    for d in range(1, Y):
        pl.semaphore_signal(barrier, inc=1, device_id=at_y(turn(y, d, Y)), device_id_type=MESH)
    for d in range(1, X):
        pl.semaphore_signal(
            barrier, inc=1, device_id=at_x(turn(x, d, X), core), device_id_type=MESH
        )
    pl.semaphore_signal(barrier, inc=1, device_id=at_x(x, mate), device_id_type=MESH)
    fixed = (Y - 1) + (X - 1) + 1
    pl.semaphore_wait(
        barrier, fixed + jnp.where(z < Z - 1, 1, 0) + jnp.where(z > 0, 1, 0)
    )

    for d in range(1, Y):
        ask_copy(d).start()
    for k in range(min(2, chunks)):
        send_own(k)
    if resident:
        for p in range(owners):
            load_dense(p, p, p).start()
    for copy in load_weights():
        copy.start()
    for d in range(1, Y):
        ask_copy(d).wait_recv()

    def gather(k):
        send_y(k, z)
        for h in range(1, Z):

            @pl.when(z >= h)
            def _():
                to_right(k, z - h).wait_recv()

                @pl.when(z < Z - 1)
                def _():
                    to_right(k, z - h).start()

            @pl.when(z + h < Z)
            def _():
                to_left(k, z + h).wait_recv()

                @pl.when(z > 0)
                def _():
                    to_left(k, z + h).start()

            @pl.when(z >= h)
            def _():
                send_y(k, z - h)

            @pl.when(z + h < Z)
            def _():
                send_y(k, z + h)

        @pl.when(k + 2 < chunks)
        def _():
            send_own(k + 2)

    def multiply(k):
        for source in range(Z):
            for j in range(J):
                entry = (source * Y + y) * J + j
                pool[pl.ds(pl.multiple_of(entry * edge, edge), edge), :] = pick(
                    k, source, wanted[pl.ds(entry, 1), :]
                ).astype(jnp.bfloat16)
        for d in range(1, Y):
            for source in range(Z):
                y_copy(k, d, source).wait_recv()
                entry = (source * Y + turn(y, d, Y)) * J
                pool[pl.ds(pl.multiple_of(entry * edge, J * edge), J * edge), :] = yrecv_buf[
                    k, d - 1, source
                ].astype(jnp.bfloat16)
        for which in (mate, core):

            def one(other, carry):
                p = other * 2 + which
                if resident:

                    @pl.when(k == 0)
                    def _():
                        load_dense(p, p, p).wait()

                    slot = p
                else:
                    load_dense(p, 0, 0).start()
                    load_dense(p, 0, 0).wait()
                    slot = 0
                partial[k, p] = jnp.dot(
                    panels[slot], pool[...], preferred_element_type=jnp.float32
                )
                if which is mate:
                    core_copy(k, other).start()
                return carry

            lax.fori_loop(0, X, one, 0)

    def reduce(k):
        for d in [*range(1, X), 0]:
            other = turn(x, d, X)
            core_copy(k, other).wait_recv()
            mine = other * 2 + core
            partial[k, mine] = partial[k, mine] + core_buf[k, other]
            if d:
                x_copy(k, d).start()

    def finish(k):
        total = partial[k, col]
        for d in range(1, X):
            x_copy(k, d).wait_recv()
            total = total + x_buf[k, d - 1]
        value = (1.0 + gin_epsilon) * zbuf[k, z] + total
        mixed[:, pl.ds(pl.multiple_of(k * width, width), width)] = value.astype(jnp.bfloat16)

    def stage(k, carry):
        @pl.when(k < chunks)
        def _():
            gather(k)

        @pl.when((k >= 2) & (k - 2 < chunks))
        def _():
            reduce(k - 2)

        @pl.when(k >= 3)
        def _():
            finish(k - 3)

        @pl.when((k >= 1) & (k - 1 < chunks))
        def _():
            multiply(k - 1)

        return carry

    lax.fori_loop(0, chunks + 3, stage, 0)

    for copy in load_weights():
        copy.wait()
    hidden_total = w_in_v.shape[1]
    step = math.gcd(512, hidden_total)
    result = jnp.broadcast_to(bias_out[...], (nodes, w_out_v.shape[1]))
    for h in range(hidden_total // step):
        part = pl.ds(h * step, step)
        hidden = jnp.dot(mixed[...], w_in_v[:, part], preferred_element_type=jnp.float32)
        hidden = jnp.maximum(hidden + bias_in[:, part], 0.0).astype(jnp.bfloat16)
        result = result + jnp.dot(hidden, w_out_v[part, :], preferred_element_type=jnp.float32)
    out[...] = result.astype(jnp.bfloat16)

    def drain(k, carry):
        for source in range(Z):

            @pl.when((z < Z - 1) & (z >= source))
            def _():
                to_right(k, source).wait_send()

            @pl.when((z > 0) & (z <= source))
            def _():
                to_left(k, source).wait_send()

            for d in range(1, Y):
                y_copy(k, d, source).wait_send()
        for other in range(X):
            core_copy(k, other).wait_send()
        for d in range(1, X):
            x_copy(k, d).wait_send()
        return carry

    lax.fori_loop(0, chunks, drain, 0)
    for d in range(1, Y):
        ask_copy(d).wait_send()


def layer(features, wanted, dense, w_in, bias_in, w_out, bias_out, edge):
    nodes, feat = features.shape
    grid_rows, J = wanted.shape
    cols = lax.axis_size("col")
    Y = max(d for d in range(1, math.isqrt(grid_rows) + 1) if grid_rows % d == 0)
    Z = grid_rows // Y
    X = cols // 2
    B = nodes // edge
    width = 128
    C = feat // width
    owners = 2 * X
    depth = dense.shape[1]
    hid = w_in.shape[1]
    resident = dense.size * 2 <= 16 * MIB
    slots = owners if resident else 1
    cfg = (Z, Y, X, J, B, edge, width, C, resident)
    names = jnp.broadcast_to(wanted.reshape(grid_rows * J, 1), (grid_rows * J, width))
    f32, bf16 = jnp.float32, jnp.bfloat16
    dma = pltpu.SemaphoreType.DMA
    y_peers, x_peers = max(Y - 1, 1), max(X - 1, 1)
    vmem = pl.BlockSpec(memory_space=pltpu.VMEM)
    hbm = pl.BlockSpec(memory_space=pl.ANY)
    return pl.pallas_call(
        functools.partial(layer_kernel, cfg),
        out_shape=jax.ShapeDtypeStruct((nodes, feat), bf16),
        in_specs=[hbm, vmem, hbm, hbm, vmem, hbm, vmem],
        out_specs=vmem,
        scratch_shapes=[
            pltpu.VMEM((C, Z, nodes, width), f32),
            pltpu.VMEM((C, y_peers, Z, J * edge, width), f32),
            pltpu.VMEM((C, y_peers, Z, J * edge, width), f32),
            pltpu.VMEM((y_peers, grid_rows * J, width), jnp.int32),
            pltpu.VMEM((slots, nodes, depth), bf16),
            pltpu.VMEM((depth, width), bf16),
            pltpu.VMEM((C, owners, nodes, width), f32),
            pltpu.VMEM((C, X, nodes, width), f32),
            pltpu.VMEM((C, x_peers, nodes, width), f32),
            pltpu.VMEM(w_in.shape, bf16),
            pltpu.VMEM(w_out.shape, bf16),
            pltpu.VMEM((nodes, feat), bf16),
            dma((C,)),
            dma((slots,)),
            dma((2,)),
            dma((C, Z)),
            dma((C, Z)),
            dma((C, Z)),
            dma((C, y_peers, Z)),
            dma((C, y_peers, Z)),
            dma((y_peers,)),
            dma((y_peers,)),
            dma((C, X)),
            dma((C, X)),
            dma((C, x_peers)),
            dma((C, x_peers)),
        ],
        compiler_params=pltpu.CompilerParams(
            collective_id=0, has_side_effects=True, vmem_limit_bytes=56 * MIB
        ),
        name="layer",
    )(features, names, dense, w_in, bias_in.reshape(1, hid), w_out, bias_out.reshape(1, feat))


def on_device(
    features, tiles, tile_rows, tile_cols, tile_count, needed, w_in, bias_in, w_out, bias_out
):
    edge = tiles.shape[-1]
    targets = lax.axis_size("col") * (features.shape[0] // edge)
    wanted = needed[0, 0]
    dense = assemble(
        tiles[0, 0], tile_rows[0, 0], tile_cols[0, 0], tile_count[0], targets, wanted.size
    )
    return layer(features, wanted, dense, w_in, bias_in, w_out, bias_out, edge)


def solution(mesh):
    placed = (
        P(("row", "col"), None),
        P("row", "col", None, None, None),
        P("row", "col", None),
        P("row", "col", None),
        P("row", "col"),
        P("row", "col", None, None),
        P(),
        P(),
        P(),
        P(),
    )
    return jax.shard_map(
        on_device, mesh=mesh, in_specs=placed, out_specs=P(("row", "col"), None), check_vma=False
    )
```

```python
import functools
import math

import jax
import jax.numpy as jnp
from jax import lax
from jax.experimental import pallas as pl
from jax.experimental.pallas import tpu as pltpu
from jax.sharding import PartitionSpec as P

gin_epsilon = 0.25
MESH = pl.DeviceIdType.MESH
MIB = 1 << 20


def assemble_kernel(rows, cols, count, tiles_ref, out_ref, acc):
    edge = tiles_ref.shape[-1]
    group = acc.shape[0] // edge
    first = pl.program_id(0) * group
    acc[...] = jnp.zeros_like(acc)

    def add(t, carry):
        local = rows[t] - first

        @pl.when((local >= 0) & (local < group))
        def _():
            at_row = pl.multiple_of(local * edge, edge)
            at_col = pl.multiple_of(cols[t] * edge, edge)
            acc[pl.ds(at_row, edge), pl.ds(at_col, edge)] += tiles_ref[t]

        return carry

    lax.fori_loop(0, count[0], add, 0)
    out_ref[...] = acc[...].astype(jnp.bfloat16)


def assemble(tiles, rows, cols, count, targets, slots):
    total, edge, _ = tiles.shape
    groups = max(1, targets * slots * edge * edge * 4 // (8 * MIB))
    height = targets // groups * edge
    return pl.pallas_call(
        assemble_kernel,
        out_shape=jax.ShapeDtypeStruct((targets * edge, slots * edge), jnp.bfloat16),
        grid_spec=pltpu.PrefetchScalarGridSpec(
            num_scalar_prefetch=3,
            grid=(groups,),
            in_specs=[pl.BlockSpec(memory_space=pltpu.VMEM)],
            out_specs=pl.BlockSpec((height, slots * edge), lambda g, *_: (g, 0)),
            scratch_shapes=[pltpu.VMEM((height, slots * edge), jnp.float32)],
        ),
        compiler_params=pltpu.CompilerParams(vmem_limit_bytes=40 * MIB),
        cost_estimate=pl.CostEstimate(
            flops=0, bytes_accessed=8 * targets * slots * edge * edge, transcendentals=0
        ),
        name="assemble",
    )(rows, cols, count, tiles)


def layer_kernel(
    cfg,
    features,
    from_left,
    from_right,
    wanted,
    dense,
    w_in,
    bias_in,
    w_out,
    bias_out,
    out,
    zbuf,
    ysend_buf,
    yrecv_buf,
    asked,
    panels,
    pool,
    partial,
    core_buf,
    x_buf,
    w_in_v,
    w_out_v,
    mixed,
    feat_sem,
    dense_sem,
    w_sem,
    z_recv,
    right_send,
    left_send,
    y_send,
    y_recv,
    ask_send,
    ask_recv,
    core_send,
    core_recv,
    x_send,
    x_recv,
):
    Z, Y, X, J, B, edge, width, chunks, resident = cfg
    owners = 2 * X
    nodes = B * edge
    row, col = lax.axis_index("row"), lax.axis_index("col")
    z, y = row // Y, lax.rem(row, Y)
    x, core = col // 2, lax.rem(col, 2)
    mate = 1 - core

    def turn(base, step, size):
        return lax.rem(base + step + size, size)

    def at_z(other):
        return (other * Y + y, col)

    def at_y(other):
        return (z * Y + other, col)

    def at_x(other, which):
        return (row, other * 2 + which)

    def local_copy(k, which):
        return pltpu.make_async_copy(
            (features, from_left, from_right)[which].at[
                :, pl.ds(pl.multiple_of(k * width, width), width)
            ],
            zbuf.at[k, (z, z - 1, z + 1)[which]],
            feat_sem.at[which, k],
        )

    def z_copy(k, source, to, sem):
        return pltpu.make_async_remote_copy(
            src_ref=zbuf.at[k, source],
            dst_ref=zbuf.at[k, source],
            send_sem=sem.at[k, source],
            recv_sem=z_recv.at[k, source],
            device_id=at_z(to),
            device_id_type=MESH,
        )

    def to_right(k, source):
        return z_copy(k, source, z + 1, right_send)

    def to_left(k, source):
        return z_copy(k, source, z - 1, left_send)

    def ask_copy(d):
        return pltpu.make_async_remote_copy(
            src_ref=wanted,
            dst_ref=asked.at[d - 1],
            send_sem=ask_send.at[d - 1],
            recv_sem=ask_recv.at[d - 1],
            device_id=at_y(turn(y, d, Y)),
            device_id_type=MESH,
        )

    def y_copy(k, d, source):
        return pltpu.make_async_remote_copy(
            src_ref=ysend_buf.at[k, d - 1, source],
            dst_ref=yrecv_buf.at[k, d - 1, source],
            send_sem=y_send.at[k, d - 1, source],
            recv_sem=y_recv.at[k, d - 1, source],
            device_id=at_y(turn(y, -d, Y)),
            device_id_type=MESH,
        )

    def core_copy(k, other):
        return pltpu.make_async_remote_copy(
            src_ref=partial.at[k, other * 2 + mate],
            dst_ref=core_buf.at[k, other],
            send_sem=core_send.at[k, other],
            recv_sem=core_recv.at[k, other],
            device_id=at_x(x, mate),
            device_id_type=MESH,
        )

    def x_copy(k, d):
        other = turn(x, d, X)
        return pltpu.make_async_remote_copy(
            src_ref=partial.at[k, other * 2 + core],
            dst_ref=x_buf.at[k, d - 1],
            send_sem=x_send.at[k, d - 1],
            recv_sem=x_recv.at[k, d - 1],
            device_id=at_x(other, core),
            device_id_type=MESH,
        )

    def load_dense(p, slot, sem):
        return pltpu.make_async_copy(
            dense.at[pl.ds(p * nodes, nodes), :], panels.at[slot], dense_sem.at[sem]
        )

    def load_weights():
        return (
            pltpu.make_async_copy(w_in, w_in_v, w_sem.at[0]),
            pltpu.make_async_copy(w_out, w_out_v, w_sem.at[1]),
        )

    def pick(k, source, row_list):
        name = jnp.broadcast_to(row_list, (edge, width))
        value = zbuf[k, source, pl.ds(0, edge), :]
        for b in range(1, B):
            value = jnp.where(name == b, zbuf[k, source, pl.ds(b * edge, edge), :], value)
        return value

    def send_y(k, source):
        for d in range(1, Y):
            for j in range(J):
                entry = (source * Y + y) * J + j
                ysend_buf[k, d - 1, source, pl.ds(j * edge, edge), :] = pick(
                    k, source, asked[d - 1, pl.ds(entry, 1), :]
                )
            y_copy(k, d, source).start()

    has_left, has_right = z > 0, z < Z - 1
    for k in range(chunks):

        @pl.when(has_left)
        def _():
            local_copy(k, 1).start()

        @pl.when(has_right)
        def _():
            local_copy(k, 2).start()

    for k in range(chunks):
        local_copy(k, 0).start()
    barrier = pltpu.get_barrier_semaphore()

    @pl.when(z < Z - 1)
    def _():
        pl.semaphore_signal(barrier, inc=1, device_id=at_z(z + 1), device_id_type=MESH)

    @pl.when(z > 0)
    def _():
        pl.semaphore_signal(barrier, inc=1, device_id=at_z(z - 1), device_id_type=MESH)

    for d in range(1, Y):
        pl.semaphore_signal(barrier, inc=1, device_id=at_y(turn(y, d, Y)), device_id_type=MESH)
    for d in range(1, X):
        pl.semaphore_signal(
            barrier, inc=1, device_id=at_x(turn(x, d, X), core), device_id_type=MESH
        )
    pl.semaphore_signal(barrier, inc=1, device_id=at_x(x, mate), device_id_type=MESH)
    fixed = (Y - 1) + (X - 1) + 1
    pl.semaphore_wait(
        barrier, fixed + jnp.where(z < Z - 1, 1, 0) + jnp.where(z > 0, 1, 0)
    )

    for d in range(1, Y):
        ask_copy(d).start()

    def first_forward(k, carry):
        @pl.when(has_left)
        def _():
            local_copy(k, 1).wait()

            @pl.when(has_right)
            def _():
                to_right(k, z - 1).start()

        @pl.when(has_right)
        def _():
            local_copy(k, 2).wait()

            @pl.when(has_left)
            def _():
                to_left(k, z + 1).start()

        return carry

    lax.fori_loop(0, chunks, first_forward, 0)
    if resident:
        for p in range(owners):
            load_dense(p, p, p).start()
    for copy in load_weights():
        copy.start()
    for d in range(1, Y):
        ask_copy(d).wait_recv()

    def near(k, carry):
        local_copy(k, 0).wait()
        send_y(k, z)

        @pl.when(has_left)
        def _():
            send_y(k, z - 1)

        @pl.when(has_right)
        def _():
            send_y(k, z + 1)

        return carry

    lax.fori_loop(0, chunks, near, 0)

    def pass_on(k, h):
        @pl.when(z >= h)
        def _():
            to_right(k, z - h).wait_recv()

            @pl.when(has_right)
            def _():
                to_right(k, z - h).start()

        @pl.when(z + h < Z)
        def _():
            to_left(k, z + h).wait_recv()

            @pl.when(has_left)
            def _():
                to_left(k, z + h).start()

        @pl.when(z >= h)
        def _():
            send_y(k, z - h)

        @pl.when(z + h < Z)
        def _():
            send_y(k, z + h)

    def far(k, carry):
        for h in range(2, Z - 1):
            pass_on(k, h)
        return carry

    lax.fori_loop(0, chunks, far, 0)

    def gather(k):
        if Z > 2:
            pass_on(k, Z - 1)

    def multiply(k):
        for source in range(Z):
            for j in range(J):
                entry = (source * Y + y) * J + j
                pool[pl.ds(pl.multiple_of(entry * edge, edge), edge), :] = pick(
                    k, source, wanted[pl.ds(entry, 1), :]
                ).astype(jnp.bfloat16)
        for d in range(1, Y):
            for source in range(Z):
                y_copy(k, d, source).wait_recv()
                entry = (source * Y + turn(y, d, Y)) * J
                pool[pl.ds(pl.multiple_of(entry * edge, J * edge), J * edge), :] = yrecv_buf[
                    k, d - 1, source
                ].astype(jnp.bfloat16)
        def one(d, carry):
            other = turn(x, d + 1, X)
            for which in (mate, core):
                p = other * 2 + which
                if resident:

                    @pl.when(k == 0)
                    def _():
                        load_dense(p, p, p).wait()

                    slot = p
                else:
                    load_dense(p, 0, 0).start()
                    load_dense(p, 0, 0).wait()
                    slot = 0
                partial[k, p] = jnp.dot(
                    panels[slot], pool[...], preferred_element_type=jnp.float32
                )
                if which is mate:
                    core_copy(k, other).start()
            return carry

        lax.fori_loop(0, X, one, 0)

    def reduce(k):
        for d in [*range(1, X), 0]:
            other = turn(x, d, X)
            core_copy(k, other).wait_recv()
            mine = other * 2 + core
            partial[k, mine] = partial[k, mine] + core_buf[k, other]
            if d:
                x_copy(k, d).start()

    def finish(k):
        total = partial[k, col]
        for d in range(1, X):
            x_copy(k, d).wait_recv()
            total = total + x_buf[k, d - 1]
        value = (1.0 + gin_epsilon) * zbuf[k, z] + total
        mixed[:, pl.ds(pl.multiple_of(k * width, width), width)] = value.astype(jnp.bfloat16)

    def stage(k, carry):
        @pl.when(k < chunks)
        def _():
            gather(k)

        @pl.when((k >= 2) & (k - 2 < chunks))
        def _():
            reduce(k - 2)

        @pl.when(k >= 3)
        def _():
            finish(k - 3)

        @pl.when((k >= 1) & (k - 1 < chunks))
        def _():
            multiply(k - 1)

        return carry

    lax.fori_loop(0, chunks + 3, stage, 0)

    for copy in load_weights():
        copy.wait()
    hidden_total = w_in_v.shape[1]
    step = math.gcd(512, hidden_total)
    result = jnp.broadcast_to(bias_out[...], (nodes, w_out_v.shape[1]))
    for h in range(hidden_total // step):
        part = pl.ds(h * step, step)
        hidden = jnp.dot(mixed[...], w_in_v[:, part], preferred_element_type=jnp.float32)
        hidden = jnp.maximum(hidden + bias_in[:, part], 0.0).astype(jnp.bfloat16)
        result = result + jnp.dot(hidden, w_out_v[part, :], preferred_element_type=jnp.float32)
    out[...] = result.astype(jnp.bfloat16)

    def drain(k, carry):
        for source in range(Z):

            @pl.when((z < Z - 1) & (z > source))
            def _():
                to_right(k, source).wait_send()

            @pl.when((z > 0) & (z < source))
            def _():
                to_left(k, source).wait_send()

            for d in range(1, Y):
                y_copy(k, d, source).wait_send()
        for other in range(X):
            core_copy(k, other).wait_send()
        for d in range(1, X):
            x_copy(k, d).wait_send()
        return carry

    lax.fori_loop(0, chunks, drain, 0)
    for d in range(1, Y):
        ask_copy(d).wait_send()


def row_grid(grid_rows):
    inner = max(d for d in range(1, math.isqrt(grid_rows) + 1) if grid_rows % d == 0)
    return grid_rows // inner, inner


def layer(features, from_left, from_right, wanted, dense, w_in, bias_in, w_out, bias_out, edge):
    nodes, feat = features.shape
    grid_rows, J = wanted.shape
    cols = lax.axis_size("col")
    Z, Y = row_grid(grid_rows)
    X = cols // 2
    B = nodes // edge
    width = 128
    C = feat // width
    owners = 2 * X
    depth = dense.shape[1]
    hid = w_in.shape[1]
    resident = dense.size * 2 <= 16 * MIB
    slots = owners if resident else 1
    cfg = (Z, Y, X, J, B, edge, width, C, resident)
    names = jnp.broadcast_to(wanted.reshape(grid_rows * J, 1), (grid_rows * J, width))
    f32, bf16 = jnp.float32, jnp.bfloat16
    dma = pltpu.SemaphoreType.DMA
    y_peers, x_peers = max(Y - 1, 1), max(X - 1, 1)
    vmem = pl.BlockSpec(memory_space=pltpu.VMEM)
    hbm = pl.BlockSpec(memory_space=pl.ANY)
    return pl.pallas_call(
        functools.partial(layer_kernel, cfg),
        out_shape=jax.ShapeDtypeStruct((nodes, feat), bf16),
        in_specs=[hbm, vmem, vmem, vmem, hbm, hbm, vmem, hbm, vmem],
        out_specs=vmem,
        scratch_shapes=[
            pltpu.VMEM((C, Z, nodes, width), f32),
            pltpu.VMEM((C, y_peers, Z, J * edge, width), f32),
            pltpu.VMEM((C, y_peers, Z, J * edge, width), f32),
            pltpu.VMEM((y_peers, grid_rows * J, width), jnp.int32),
            pltpu.VMEM((slots, nodes, depth), bf16),
            pltpu.VMEM((depth, width), bf16),
            pltpu.VMEM((C, owners, nodes, width), f32),
            pltpu.VMEM((C, X, nodes, width), f32),
            pltpu.VMEM((C, x_peers, nodes, width), f32),
            pltpu.VMEM(w_in.shape, bf16),
            pltpu.VMEM(w_out.shape, bf16),
            pltpu.VMEM((nodes, feat), bf16),
            dma((3, C)),
            dma((slots,)),
            dma((2,)),
            dma((C, Z)),
            dma((C, Z)),
            dma((C, Z)),
            dma((C, y_peers, Z)),
            dma((C, y_peers, Z)),
            dma((y_peers,)),
            dma((y_peers,)),
            dma((C, X)),
            dma((C, X)),
            dma((C, x_peers)),
            dma((C, x_peers)),
        ],
        compiler_params=pltpu.CompilerParams(
            collective_id=0, has_side_effects=True, vmem_limit_bytes=(40 if resident else 56) * MIB
        ),
        name="layer",
    )(features, from_left, from_right, names, dense, w_in, bias_in.reshape(1, hid), w_out, bias_out.reshape(1, feat))


def on_device(
    features, tiles, tile_rows, tile_cols, tile_count, needed, w_in, bias_in, w_out, bias_out
):
    edge = tiles.shape[-1]
    targets = lax.axis_size("col") * (features.shape[0] // edge)
    wanted = needed[0, 0]
    Z, Y = row_grid(lax.axis_size("row"))
    pairs = [(r, r + Y) for r in range((Z - 1) * Y)]
    from_left = lax.ppermute(features, "row", pairs)
    from_right = lax.ppermute(features, "row", [(b, a) for a, b in pairs])
    dense = assemble(
        tiles[0, 0], tile_rows[0, 0], tile_cols[0, 0], tile_count[0], targets, wanted.size
    )
    return layer(features, from_left, from_right, wanted, dense, w_in, bias_in, w_out, bias_out, edge)


def solution(mesh):
    placed = (
        P(("row", "col"), None),
        P("row", "col", None, None, None),
        P("row", "col", None),
        P("row", "col", None),
        P("row", "col"),
        P("row", "col", None, None),
        P(),
        P(),
        P(),
        P(),
    )
    return jax.shard_map(
        on_device, mesh=mesh, in_specs=placed, out_specs=P(("row", "col"), None), check_vma=False
    )
```

```python
import functools
import math

import jax
import jax.numpy as jnp
from jax import lax
from jax.experimental import pallas as pl
from jax.experimental.pallas import tpu as pltpu
from jax.sharding import PartitionSpec as P

gin_epsilon = 0.25
MESH = pl.DeviceIdType.MESH
MIB = 1 << 20


def assemble_kernel(rows, cols, count, tiles_ref, out_ref, acc):
    edge = tiles_ref.shape[-1]
    group = acc.shape[0] // edge
    first = pl.program_id(0) * group
    acc[...] = jnp.zeros_like(acc)

    def add(t, carry):
        local = rows[t] - first

        @pl.when((local >= 0) & (local < group))
        def _():
            at_row = pl.multiple_of(local * edge, edge)
            at_col = pl.multiple_of(cols[t] * edge, edge)
            acc[pl.ds(at_row, edge), pl.ds(at_col, edge)] += tiles_ref[t]

        return carry

    lax.fori_loop(0, count[0], add, 0)
    out_ref[...] = acc[...].astype(jnp.bfloat16)


def assemble(tiles, rows, cols, count, targets, slots):
    total, edge, _ = tiles.shape
    groups = max(1, targets * slots * edge * edge * 4 // (8 * MIB))
    height = targets // groups * edge
    return pl.pallas_call(
        assemble_kernel,
        out_shape=jax.ShapeDtypeStruct((targets * edge, slots * edge), jnp.bfloat16),
        grid_spec=pltpu.PrefetchScalarGridSpec(
            num_scalar_prefetch=3,
            grid=(groups,),
            in_specs=[pl.BlockSpec(memory_space=pltpu.VMEM)],
            out_specs=pl.BlockSpec((height, slots * edge), lambda g, *_: (g, 0)),
            scratch_shapes=[pltpu.VMEM((height, slots * edge), jnp.float32)],
        ),
        compiler_params=pltpu.CompilerParams(vmem_limit_bytes=40 * MIB),
        cost_estimate=pl.CostEstimate(
            flops=0, bytes_accessed=8 * targets * slots * edge * edge, transcendentals=0
        ),
        name="assemble",
    )(rows, cols, count, tiles)


def layer_kernel(
    cfg,
    features,
    from_left,
    from_right,
    wanted,
    dense,
    w_in,
    bias_in,
    w_out,
    bias_out,
    out,
    zbuf,
    ysend_buf,
    yrecv_buf,
    asked,
    panels,
    pool,
    partial,
    core_buf,
    x_buf,
    w_in_v,
    w_out_v,
    mixed,
    feat_sem,
    dense_sem,
    w_sem,
    z_recv,
    right_send,
    left_send,
    y_send,
    y_recv,
    ask_send,
    ask_recv,
    core_send,
    core_recv,
    x_send,
    x_recv,
):
    Z, Y, X, J, B, edge, width, chunks, resident = cfg
    owners = 2 * X
    nodes = B * edge
    row, col = lax.axis_index("row"), lax.axis_index("col")
    z, y = row // Y, lax.rem(row, Y)
    x, core = col // 2, lax.rem(col, 2)
    mate = 1 - core

    def turn(base, step, size):
        return lax.rem(base + step + size, size)

    def at_z(other):
        return (other * Y + y, col)

    def at_y(other):
        return (z * Y + other, col)

    def at_x(other, which):
        return (row, other * 2 + which)

    def local_copy(k, which):
        return pltpu.make_async_copy(
            (features, from_left, from_right)[which].at[
                :, pl.ds(pl.multiple_of(k * width, width), width)
            ],
            zbuf.at[k, (z, z - 1, z + 1)[which]],
            feat_sem.at[which, k],
        )

    def z_copy(k, source, to, sem):
        return pltpu.make_async_remote_copy(
            src_ref=zbuf.at[k, source],
            dst_ref=zbuf.at[k, source],
            send_sem=sem.at[k, source],
            recv_sem=z_recv.at[k, source],
            device_id=at_z(to),
            device_id_type=MESH,
        )

    def to_right(k, source):
        return z_copy(k, source, z + 1, right_send)

    def to_left(k, source):
        return z_copy(k, source, z - 1, left_send)

    def ask_copy(d):
        return pltpu.make_async_remote_copy(
            src_ref=wanted,
            dst_ref=asked.at[d - 1],
            send_sem=ask_send.at[d - 1],
            recv_sem=ask_recv.at[d - 1],
            device_id=at_y(turn(y, d, Y)),
            device_id_type=MESH,
        )

    def y_copy(k, d, source):
        return pltpu.make_async_remote_copy(
            src_ref=ysend_buf.at[k, d - 1, source],
            dst_ref=yrecv_buf.at[k, d - 1, source],
            send_sem=y_send.at[k, d - 1, source],
            recv_sem=y_recv.at[k, d - 1, source],
            device_id=at_y(turn(y, -d, Y)),
            device_id_type=MESH,
        )

    def core_copy(k, other):
        return pltpu.make_async_remote_copy(
            src_ref=partial.at[k, other * 2 + mate],
            dst_ref=core_buf.at[k, other],
            send_sem=core_send.at[k, other],
            recv_sem=core_recv.at[k, other],
            device_id=at_x(x, mate),
            device_id_type=MESH,
        )

    def x_copy(k, d):
        other = turn(x, d, X)
        return pltpu.make_async_remote_copy(
            src_ref=partial.at[k, other * 2 + core],
            dst_ref=x_buf.at[k, d - 1],
            send_sem=x_send.at[k, d - 1],
            recv_sem=x_recv.at[k, d - 1],
            device_id=at_x(other, core),
            device_id_type=MESH,
        )

    def load_dense(p, slot, sem):
        return pltpu.make_async_copy(
            dense.at[pl.ds(p * nodes, nodes), :], panels.at[slot], dense_sem.at[sem]
        )

    def load_weights():
        return (
            pltpu.make_async_copy(w_in, w_in_v, w_sem.at[0]),
            pltpu.make_async_copy(w_out, w_out_v, w_sem.at[1]),
        )

    def pick(k, source, row_list):
        name = jnp.broadcast_to(row_list, (edge, width))
        value = zbuf[k, source, pl.ds(0, edge), :]
        for b in range(1, B):
            value = jnp.where(name == b, zbuf[k, source, pl.ds(b * edge, edge), :], value)
        return value

    def send_y(k, source):
        for d in range(1, Y):
            for j in range(J):
                entry = (source * Y + y) * J + j
                ysend_buf[k, d - 1, source, pl.ds(j * edge, edge), :] = pick(
                    k, source, asked[d - 1, pl.ds(entry, 1), :]
                )
            y_copy(k, d, source).start()

    has_left, has_right = z > 0, z < Z - 1
    for k in range(chunks):

        @pl.when(has_left)
        def _():
            local_copy(k, 1).start()

        @pl.when(has_right)
        def _():
            local_copy(k, 2).start()

    for k in range(chunks):
        local_copy(k, 0).start()
    barrier = pltpu.get_barrier_semaphore()

    @pl.when(z < Z - 1)
    def _():
        pl.semaphore_signal(barrier, inc=1, device_id=at_z(z + 1), device_id_type=MESH)

    @pl.when(z > 0)
    def _():
        pl.semaphore_signal(barrier, inc=1, device_id=at_z(z - 1), device_id_type=MESH)

    for d in range(1, Y):
        pl.semaphore_signal(barrier, inc=1, device_id=at_y(turn(y, d, Y)), device_id_type=MESH)
    for d in range(1, X):
        pl.semaphore_signal(
            barrier, inc=1, device_id=at_x(turn(x, d, X), core), device_id_type=MESH
        )
    pl.semaphore_signal(barrier, inc=1, device_id=at_x(x, mate), device_id_type=MESH)
    fixed = (Y - 1) + (X - 1) + 1
    pl.semaphore_wait(
        barrier, fixed + jnp.where(z < Z - 1, 1, 0) + jnp.where(z > 0, 1, 0)
    )

    for d in range(1, Y):
        ask_copy(d).start()

    def first_forward(k):
        @pl.when(has_left)
        def _():
            local_copy(k, 1).wait()

            @pl.when(has_right)
            def _():
                to_right(k, z - 1).start()

        @pl.when(has_right)
        def _():
            local_copy(k, 2).wait()

            @pl.when(has_left)
            def _():
                to_left(k, z + 1).start()

    for k in range(min(2, chunks)):
        first_forward(k)
    if resident:
        for p in range(owners):
            load_dense(p, p, p).start()
    for copy in load_weights():
        copy.start()
    for d in range(1, Y):
        ask_copy(d).wait_recv()

    def near(k):
        local_copy(k, 0).wait()
        send_y(k, z)

        @pl.when(has_left)
        def _():
            send_y(k, z - 1)

        @pl.when(has_right)
        def _():
            send_y(k, z + 1)

    def pass_on(k, h):
        @pl.when(z >= h)
        def _():
            to_right(k, z - h).wait_recv()

            @pl.when(has_right)
            def _():
                to_right(k, z - h).start()

        @pl.when(z + h < Z)
        def _():
            to_left(k, z + h).wait_recv()

            @pl.when(has_left)
            def _():
                to_left(k, z + h).start()

        @pl.when(z >= h)
        def _():
            send_y(k, z - h)

        @pl.when(z + h < Z)
        def _():
            send_y(k, z + h)

    def far(k):
        for h in range(2, Z):
            pass_on(k, h)

        @pl.when(k + 2 < chunks)
        def _():
            first_forward(k + 2)

    def multiply(k):
        for source in range(Z):
            for j in range(J):
                entry = (source * Y + y) * J + j
                pool[pl.ds(pl.multiple_of(entry * edge, edge), edge), :] = pick(
                    k, source, wanted[pl.ds(entry, 1), :]
                ).astype(jnp.bfloat16)
        for d in range(1, Y):
            for source in range(Z):
                y_copy(k, d, source).wait_recv()
                entry = (source * Y + turn(y, d, Y)) * J
                pool[pl.ds(pl.multiple_of(entry * edge, J * edge), J * edge), :] = yrecv_buf[
                    k, d - 1, source
                ].astype(jnp.bfloat16)
        def one(d, carry):
            other = turn(x, d + 1, X)
            for which in (mate, core):
                p = other * 2 + which
                if resident:

                    @pl.when(k == 0)
                    def _():
                        load_dense(p, p, p).wait()

                    slot = p
                else:
                    load_dense(p, 0, 0).start()
                    load_dense(p, 0, 0).wait()
                    slot = 0
                partial[k, p] = jnp.dot(
                    panels[slot], pool[...], preferred_element_type=jnp.float32
                )
                if which is mate:
                    core_copy(k, other).start()
            return carry

        lax.fori_loop(0, X, one, 0)

    def reduce(k):
        for d in [*range(1, X), 0]:
            other = turn(x, d, X)
            core_copy(k, other).wait_recv()
            mine = other * 2 + core
            partial[k, mine] = partial[k, mine] + core_buf[k, other]
            if d:
                x_copy(k, d).start()

    def finish(k):
        total = partial[k, col]
        for d in range(1, X):
            x_copy(k, d).wait_recv()
            total = total + x_buf[k, d - 1]
        value = (1.0 + gin_epsilon) * zbuf[k, z] + total
        mixed[:, pl.ds(pl.multiple_of(k * width, width), width)] = value.astype(jnp.bfloat16)

    def stage(k, carry):
        @pl.when(k < chunks)
        def _():
            near(k)

        @pl.when((k >= 1) & (k - 1 < chunks))
        def _():
            multiply(k - 1)
            reduce(k - 1)

        @pl.when(k < chunks)
        def _():
            far(k)

        @pl.when(k >= 2)
        def _():
            finish(k - 2)

        return carry

    lax.fori_loop(0, chunks + 2, stage, 0)

    for copy in load_weights():
        copy.wait()
    hidden_total = w_in_v.shape[1]
    step = math.gcd(512, hidden_total)
    result = jnp.broadcast_to(bias_out[...], (nodes, w_out_v.shape[1]))
    for h in range(hidden_total // step):
        part = pl.ds(h * step, step)
        hidden = jnp.dot(mixed[...], w_in_v[:, part], preferred_element_type=jnp.float32)
        hidden = jnp.maximum(hidden + bias_in[:, part], 0.0).astype(jnp.bfloat16)
        result = result + jnp.dot(hidden, w_out_v[part, :], preferred_element_type=jnp.float32)
    out[...] = result.astype(jnp.bfloat16)

    def drain(k, carry):
        for source in range(Z):

            @pl.when((z < Z - 1) & (z > source))
            def _():
                to_right(k, source).wait_send()

            @pl.when((z > 0) & (z < source))
            def _():
                to_left(k, source).wait_send()

            for d in range(1, Y):
                y_copy(k, d, source).wait_send()
        for other in range(X):
            core_copy(k, other).wait_send()
        for d in range(1, X):
            x_copy(k, d).wait_send()
        return carry

    lax.fori_loop(0, chunks, drain, 0)
    for d in range(1, Y):
        ask_copy(d).wait_send()


def row_grid(grid_rows):
    inner = max(d for d in range(1, math.isqrt(grid_rows) + 1) if grid_rows % d == 0)
    return grid_rows // inner, inner


def layer(features, from_left, from_right, wanted, dense, w_in, bias_in, w_out, bias_out, edge):
    nodes, feat = features.shape
    grid_rows, J = wanted.shape
    cols = lax.axis_size("col")
    Z, Y = row_grid(grid_rows)
    X = cols // 2
    B = nodes // edge
    width = 128
    C = feat // width
    owners = 2 * X
    depth = dense.shape[1]
    hid = w_in.shape[1]
    resident = dense.size * 2 <= 16 * MIB
    slots = owners if resident else 1
    cfg = (Z, Y, X, J, B, edge, width, C, resident)
    names = jnp.broadcast_to(wanted.reshape(grid_rows * J, 1), (grid_rows * J, width))
    f32, bf16 = jnp.float32, jnp.bfloat16
    dma = pltpu.SemaphoreType.DMA
    y_peers, x_peers = max(Y - 1, 1), max(X - 1, 1)
    vmem = pl.BlockSpec(memory_space=pltpu.VMEM)
    hbm = pl.BlockSpec(memory_space=pl.ANY)
    return pl.pallas_call(
        functools.partial(layer_kernel, cfg),
        out_shape=jax.ShapeDtypeStruct((nodes, feat), bf16),
        in_specs=[hbm, vmem, vmem, vmem, hbm, hbm, vmem, hbm, vmem],
        out_specs=vmem,
        scratch_shapes=[
            pltpu.VMEM((C, Z, nodes, width), f32),
            pltpu.VMEM((C, y_peers, Z, J * edge, width), f32),
            pltpu.VMEM((C, y_peers, Z, J * edge, width), f32),
            pltpu.VMEM((y_peers, grid_rows * J, width), jnp.int32),
            pltpu.VMEM((slots, nodes, depth), bf16),
            pltpu.VMEM((depth, width), bf16),
            pltpu.VMEM((C, owners, nodes, width), f32),
            pltpu.VMEM((C, X, nodes, width), f32),
            pltpu.VMEM((C, x_peers, nodes, width), f32),
            pltpu.VMEM(w_in.shape, bf16),
            pltpu.VMEM(w_out.shape, bf16),
            pltpu.VMEM((nodes, feat), bf16),
            dma((3, C)),
            dma((slots,)),
            dma((2,)),
            dma((C, Z)),
            dma((C, Z)),
            dma((C, Z)),
            dma((C, y_peers, Z)),
            dma((C, y_peers, Z)),
            dma((y_peers,)),
            dma((y_peers,)),
            dma((C, X)),
            dma((C, X)),
            dma((C, x_peers)),
            dma((C, x_peers)),
        ],
        compiler_params=pltpu.CompilerParams(
            collective_id=0, has_side_effects=True, vmem_limit_bytes=(40 if resident else 56) * MIB
        ),
        name="layer",
    )(features, from_left, from_right, names, dense, w_in, bias_in.reshape(1, hid), w_out, bias_out.reshape(1, feat))


def on_device(
    features, tiles, tile_rows, tile_cols, tile_count, needed, w_in, bias_in, w_out, bias_out
):
    edge = tiles.shape[-1]
    targets = lax.axis_size("col") * (features.shape[0] // edge)
    wanted = needed[0, 0]
    Z, Y = row_grid(lax.axis_size("row"))
    pairs = [(r, r + Y) for r in range((Z - 1) * Y)]
    from_left = lax.ppermute(features, "row", pairs)
    from_right = lax.ppermute(features, "row", [(b, a) for a, b in pairs])
    dense = assemble(
        tiles[0, 0], tile_rows[0, 0], tile_cols[0, 0], tile_count[0], targets, wanted.size
    )
    return layer(features, from_left, from_right, wanted, dense, w_in, bias_in, w_out, bias_out, edge)


def solution(mesh):
    placed = (
        P(("row", "col"), None),
        P("row", "col", None, None, None),
        P("row", "col", None),
        P("row", "col", None),
        P("row", "col"),
        P("row", "col", None, None),
        P(),
        P(),
        P(),
        P(),
    )
    return jax.shard_map(
        on_device, mesh=mesh, in_specs=placed, out_specs=P(("row", "col"), None), check_vma=False
    )
```

```python
import functools
import math

import jax
import jax.numpy as jnp
from jax import lax
from jax.experimental import pallas as pl
from jax.experimental.pallas import tpu as pltpu
from jax.sharding import PartitionSpec as P

gin_epsilon = 0.25
MESH = pl.DeviceIdType.MESH
MIB = 1 << 20


def assemble_kernel(rows, cols, count, tiles_ref, out_ref, acc):
    edge = tiles_ref.shape[-1]
    group = acc.shape[0] // edge
    first = pl.program_id(0) * group
    acc[...] = jnp.zeros_like(acc)

    def add(t, carry):
        local = rows[t] - first

        @pl.when((local >= 0) & (local < group))
        def _():
            at_row = pl.multiple_of(local * edge, edge)
            at_col = pl.multiple_of(cols[t] * edge, edge)
            acc[pl.ds(at_row, edge), pl.ds(at_col, edge)] += tiles_ref[t]

        return carry

    lax.fori_loop(0, count[0], add, 0)
    out_ref[...] = acc[...].astype(jnp.bfloat16)


def assemble(tiles, rows, cols, count, targets, slots):
    total, edge, _ = tiles.shape
    groups = max(1, targets * slots * edge * edge * 4 // (8 * MIB))
    height = targets // groups * edge
    return pl.pallas_call(
        assemble_kernel,
        out_shape=jax.ShapeDtypeStruct((targets * edge, slots * edge), jnp.bfloat16),
        grid_spec=pltpu.PrefetchScalarGridSpec(
            num_scalar_prefetch=3,
            grid=(groups,),
            in_specs=[pl.BlockSpec(memory_space=pltpu.VMEM)],
            out_specs=pl.BlockSpec((height, slots * edge), lambda g, *_: (g, 0)),
            scratch_shapes=[pltpu.VMEM((height, slots * edge), jnp.float32)],
        ),
        compiler_params=pltpu.CompilerParams(vmem_limit_bytes=40 * MIB),
        cost_estimate=pl.CostEstimate(
            flops=0, bytes_accessed=8 * targets * slots * edge * edge, transcendentals=0
        ),
        name="assemble",
    )(rows, cols, count, tiles)


def layer_kernel(
    cfg,
    features,
    from_left,
    from_right,
    wanted,
    dense,
    w_in,
    bias_in,
    w_out,
    bias_out,
    out,
    zbuf,
    ysend_buf,
    yrecv_buf,
    asked,
    panels,
    pool,
    partial,
    core_buf,
    x_buf,
    w_in_v,
    w_out_v,
    mixed,
    feat_sem,
    dense_sem,
    w_sem,
    z_recv,
    right_send,
    left_send,
    y_send,
    y_recv,
    ask_send,
    ask_recv,
    core_send,
    core_recv,
    x_send,
    x_recv,
):
    Z, Y, X, J, B, edge, width, chunks, resident = cfg
    owners = 2 * X
    nodes = B * edge
    row, col = lax.axis_index("row"), lax.axis_index("col")
    z, y = row // Y, lax.rem(row, Y)
    x, core = col // 2, lax.rem(col, 2)
    mate = 1 - core

    def turn(base, step, size):
        return lax.rem(base + step + size, size)

    def at_z(other):
        return (other * Y + y, col)

    def at_y(other):
        return (z * Y + other, col)

    def at_x(other, which):
        return (row, other * 2 + which)

    def local_copy(k, which):
        return pltpu.make_async_copy(
            (features, from_left, from_right)[which].at[
                :, pl.ds(pl.multiple_of(k * width, width), width)
            ],
            zbuf.at[k, (z, z - 1, z + 1)[which]],
            feat_sem.at[which, k],
        )

    def z_copy(k, source, to, sem):
        return pltpu.make_async_remote_copy(
            src_ref=zbuf.at[k, source],
            dst_ref=zbuf.at[k, source],
            send_sem=sem.at[k, source],
            recv_sem=z_recv.at[k, source],
            device_id=at_z(to),
            device_id_type=MESH,
        )

    def to_right(k, source):
        return z_copy(k, source, z + 1, right_send)

    def to_left(k, source):
        return z_copy(k, source, z - 1, left_send)

    def ask_copy(d):
        return pltpu.make_async_remote_copy(
            src_ref=wanted,
            dst_ref=asked.at[d - 1],
            send_sem=ask_send.at[d - 1],
            recv_sem=ask_recv.at[d - 1],
            device_id=at_y(turn(y, d, Y)),
            device_id_type=MESH,
        )

    def y_copy(k, d, source):
        return pltpu.make_async_remote_copy(
            src_ref=ysend_buf.at[k, d - 1, source],
            dst_ref=yrecv_buf.at[k, d - 1, source],
            send_sem=y_send.at[k, d - 1, source],
            recv_sem=y_recv.at[k, d - 1, source],
            device_id=at_y(turn(y, -d, Y)),
            device_id_type=MESH,
        )

    def core_copy(k, other):
        return pltpu.make_async_remote_copy(
            src_ref=partial.at[k, other * 2 + mate],
            dst_ref=core_buf.at[k, other],
            send_sem=core_send.at[k, other],
            recv_sem=core_recv.at[k, other],
            device_id=at_x(x, mate),
            device_id_type=MESH,
        )

    def x_copy(k, d):
        other = turn(x, d, X)
        return pltpu.make_async_remote_copy(
            src_ref=partial.at[k, other * 2 + core],
            dst_ref=x_buf.at[k, d - 1],
            send_sem=x_send.at[k, d - 1],
            recv_sem=x_recv.at[k, d - 1],
            device_id=at_x(other, core),
            device_id_type=MESH,
        )

    def load_dense(p, slot, sem):
        return pltpu.make_async_copy(
            dense.at[pl.ds(p * nodes, nodes), :], panels.at[slot], dense_sem.at[sem]
        )

    def load_weights():
        return (
            pltpu.make_async_copy(w_in, w_in_v, w_sem.at[0]),
            pltpu.make_async_copy(w_out, w_out_v, w_sem.at[1]),
        )

    def pick(k, source, row_list):
        name = jnp.broadcast_to(row_list, (edge, width))
        value = zbuf[k, source, pl.ds(0, edge), :]
        for b in range(1, B):
            value = jnp.where(name == b, zbuf[k, source, pl.ds(b * edge, edge), :], value)
        return value

    def send_y(k, source):
        for d in range(1, Y):
            for j in range(J):
                entry = (source * Y + y) * J + j
                ysend_buf[k, d - 1, source, pl.ds(j * edge, edge), :] = pick(
                    k, source, asked[d - 1, pl.ds(entry, 1), :]
                )
            y_copy(k, d, source).start()

    has_left, has_right = z > 0, z < Z - 1
    for k in range(chunks):

        @pl.when(has_left)
        def _():
            local_copy(k, 1).start()

        @pl.when(has_right)
        def _():
            local_copy(k, 2).start()

    for k in range(chunks):
        local_copy(k, 0).start()
    barrier = pltpu.get_barrier_semaphore()

    @pl.when(z < Z - 1)
    def _():
        pl.semaphore_signal(barrier, inc=1, device_id=at_z(z + 1), device_id_type=MESH)

    @pl.when(z > 0)
    def _():
        pl.semaphore_signal(barrier, inc=1, device_id=at_z(z - 1), device_id_type=MESH)

    for d in range(1, Y):
        pl.semaphore_signal(barrier, inc=1, device_id=at_y(turn(y, d, Y)), device_id_type=MESH)
    for d in range(1, X):
        pl.semaphore_signal(
            barrier, inc=1, device_id=at_x(turn(x, d, X), core), device_id_type=MESH
        )
    pl.semaphore_signal(barrier, inc=1, device_id=at_x(x, mate), device_id_type=MESH)
    fixed = (Y - 1) + (X - 1) + 1
    pl.semaphore_wait(
        barrier, fixed + jnp.where(z < Z - 1, 1, 0) + jnp.where(z > 0, 1, 0)
    )

    for d in range(1, Y):
        ask_copy(d).start()

    def first_forward(k, carry):
        @pl.when(has_left)
        def _():
            local_copy(k, 1).wait()

            @pl.when(has_right)
            def _():
                to_right(k, z - 1).start()

        @pl.when(has_right)
        def _():
            local_copy(k, 2).wait()

            @pl.when(has_left)
            def _():
                to_left(k, z + 1).start()

        return carry

    lax.fori_loop(0, chunks, first_forward, 0)
    if resident:
        for p in range(owners):
            load_dense(p, p, p).start()
    for copy in load_weights():
        copy.start()
    for d in range(1, Y):
        ask_copy(d).wait_recv()

    def near(k):
        local_copy(k, 0).wait()
        send_y(k, z)

        @pl.when(has_left)
        def _():
            send_y(k, z - 1)

        @pl.when(has_right)
        def _():
            send_y(k, z + 1)

    def pass_on(k, h):
        @pl.when(z >= h)
        def _():
            to_right(k, z - h).wait_recv()

            @pl.when(has_right)
            def _():
                to_right(k, z - h).start()

        @pl.when(z + h < Z)
        def _():
            to_left(k, z + h).wait_recv()

            @pl.when(has_left)
            def _():
                to_left(k, z + h).start()

        @pl.when(z >= h)
        def _():
            send_y(k, z - h)

        @pl.when(z + h < Z)
        def _():
            send_y(k, z + h)

    def far(k, carry):
        near(k)
        for h in range(2, Z - 1):
            pass_on(k, h)
        return carry

    lax.fori_loop(0, chunks, far, 0)

    def gather(k):
        if Z > 2:
            pass_on(k, Z - 1)

    def multiply(k):
        for source in range(Z):
            for j in range(J):
                entry = (source * Y + y) * J + j
                pool[pl.ds(pl.multiple_of(entry * edge, edge), edge), :] = pick(
                    k, source, wanted[pl.ds(entry, 1), :]
                ).astype(jnp.bfloat16)
        for d in range(1, Y):
            for source in range(Z):
                y_copy(k, d, source).wait_recv()
                entry = (source * Y + turn(y, d, Y)) * J
                pool[pl.ds(pl.multiple_of(entry * edge, J * edge), J * edge), :] = yrecv_buf[
                    k, d - 1, source
                ].astype(jnp.bfloat16)
        def one(d, carry):
            other = turn(x, d + 1, X)
            for which in (mate, core):
                p = other * 2 + which
                if resident:

                    @pl.when(k == 0)
                    def _():
                        load_dense(p, p, p).wait()

                    slot = p
                else:
                    load_dense(p, 0, 0).start()
                    load_dense(p, 0, 0).wait()
                    slot = 0
                partial[k, p] = jnp.dot(
                    panels[slot], pool[...], preferred_element_type=jnp.float32
                )
                if which is mate:
                    core_copy(k, other).start()
            return carry

        lax.fori_loop(0, X, one, 0)

    def reduce(k):
        for d in [*range(1, X), 0]:
            other = turn(x, d, X)
            core_copy(k, other).wait_recv()
            mine = other * 2 + core
            partial[k, mine] = partial[k, mine] + core_buf[k, other]
            if d:
                x_copy(k, d).start()

    def finish(k):
        total = partial[k, col]
        for d in range(1, X):
            x_copy(k, d).wait_recv()
            total = total + x_buf[k, d - 1]
        value = (1.0 + gin_epsilon) * zbuf[k, z] + total
        mixed[:, pl.ds(pl.multiple_of(k * width, width), width)] = value.astype(jnp.bfloat16)

    def stage(k, carry):
        @pl.when(k < chunks)
        def _():
            gather(k)

        @pl.when((k >= 1) & (k - 1 < chunks))
        def _():
            multiply(k - 1)
            reduce(k - 1)

        @pl.when(k >= 2)
        def _():
            finish(k - 2)

        return carry

    lax.fori_loop(0, chunks + 2, stage, 0)

    for copy in load_weights():
        copy.wait()
    hidden_total = w_in_v.shape[1]
    step = math.gcd(512, hidden_total)
    result = jnp.broadcast_to(bias_out[...], (nodes, w_out_v.shape[1]))
    for h in range(hidden_total // step):
        part = pl.ds(h * step, step)
        hidden = jnp.dot(mixed[...], w_in_v[:, part], preferred_element_type=jnp.float32)
        hidden = jnp.maximum(hidden + bias_in[:, part], 0.0).astype(jnp.bfloat16)
        result = result + jnp.dot(hidden, w_out_v[part, :], preferred_element_type=jnp.float32)
    out[...] = result.astype(jnp.bfloat16)

    def drain(k, carry):
        for source in range(Z):

            @pl.when((z < Z - 1) & (z > source))
            def _():
                to_right(k, source).wait_send()

            @pl.when((z > 0) & (z < source))
            def _():
                to_left(k, source).wait_send()

            for d in range(1, Y):
                y_copy(k, d, source).wait_send()
        for other in range(X):
            core_copy(k, other).wait_send()
        for d in range(1, X):
            x_copy(k, d).wait_send()
        return carry

    lax.fori_loop(0, chunks, drain, 0)
    for d in range(1, Y):
        ask_copy(d).wait_send()


def row_grid(grid_rows):
    inner = max(d for d in range(1, math.isqrt(grid_rows) + 1) if grid_rows % d == 0)
    return grid_rows // inner, inner


def layer(features, from_left, from_right, wanted, dense, w_in, bias_in, w_out, bias_out, edge):
    nodes, feat = features.shape
    grid_rows, J = wanted.shape
    cols = lax.axis_size("col")
    Z, Y = row_grid(grid_rows)
    X = cols // 2
    B = nodes // edge
    width = 128
    C = feat // width
    owners = 2 * X
    depth = dense.shape[1]
    hid = w_in.shape[1]
    resident = dense.size * 2 <= 16 * MIB
    slots = owners if resident else 1
    cfg = (Z, Y, X, J, B, edge, width, C, resident)
    names = jnp.broadcast_to(wanted.reshape(grid_rows * J, 1), (grid_rows * J, width))
    f32, bf16 = jnp.float32, jnp.bfloat16
    dma = pltpu.SemaphoreType.DMA
    y_peers, x_peers = max(Y - 1, 1), max(X - 1, 1)
    vmem = pl.BlockSpec(memory_space=pltpu.VMEM)
    hbm = pl.BlockSpec(memory_space=pl.ANY)
    return pl.pallas_call(
        functools.partial(layer_kernel, cfg),
        out_shape=jax.ShapeDtypeStruct((nodes, feat), bf16),
        in_specs=[hbm, vmem, vmem, vmem, hbm, hbm, vmem, hbm, vmem],
        out_specs=vmem,
        scratch_shapes=[
            pltpu.VMEM((C, Z, nodes, width), f32),
            pltpu.VMEM((C, y_peers, Z, J * edge, width), f32),
            pltpu.VMEM((C, y_peers, Z, J * edge, width), f32),
            pltpu.VMEM((y_peers, grid_rows * J, width), jnp.int32),
            pltpu.VMEM((slots, nodes, depth), bf16),
            pltpu.VMEM((depth, width), bf16),
            pltpu.VMEM((C, owners, nodes, width), f32),
            pltpu.VMEM((C, X, nodes, width), f32),
            pltpu.VMEM((C, x_peers, nodes, width), f32),
            pltpu.VMEM(w_in.shape, bf16),
            pltpu.VMEM(w_out.shape, bf16),
            pltpu.VMEM((nodes, feat), bf16),
            dma((3, C)),
            dma((slots,)),
            dma((2,)),
            dma((C, Z)),
            dma((C, Z)),
            dma((C, Z)),
            dma((C, y_peers, Z)),
            dma((C, y_peers, Z)),
            dma((y_peers,)),
            dma((y_peers,)),
            dma((C, X)),
            dma((C, X)),
            dma((C, x_peers)),
            dma((C, x_peers)),
        ],
        compiler_params=pltpu.CompilerParams(
            collective_id=0, has_side_effects=True, vmem_limit_bytes=(40 if resident else 56) * MIB
        ),
        name="layer",
    )(features, from_left, from_right, names, dense, w_in, bias_in.reshape(1, hid), w_out, bias_out.reshape(1, feat))


def on_device(
    features, tiles, tile_rows, tile_cols, tile_count, needed, w_in, bias_in, w_out, bias_out
):
    edge = tiles.shape[-1]
    targets = lax.axis_size("col") * (features.shape[0] // edge)
    wanted = needed[0, 0]
    Z, Y = row_grid(lax.axis_size("row"))
    pairs = [(r, r + Y) for r in range((Z - 1) * Y)]
    from_left = lax.ppermute(features, "row", pairs)
    from_right = lax.ppermute(features, "row", [(b, a) for a, b in pairs])
    dense = assemble(
        tiles[0, 0], tile_rows[0, 0], tile_cols[0, 0], tile_count[0], targets, wanted.size
    )
    return layer(features, from_left, from_right, wanted, dense, w_in, bias_in, w_out, bias_out, edge)


def solution(mesh):
    placed = (
        P(("row", "col"), None),
        P("row", "col", None, None, None),
        P("row", "col", None),
        P("row", "col", None),
        P("row", "col"),
        P("row", "col", None, None),
        P(),
        P(),
        P(),
        P(),
    )
    return jax.shard_map(
        on_device, mesh=mesh, in_specs=placed, out_specs=P(("row", "col"), None), check_vma=False
    )
```
